128 devices in a mesh: pipe: 4 (over z), width: 32 (over y, x, core).
Axes of the slice: x: 4, y: 4, z: 4, core: 2. Of those that a mesh axis runs over, the one named last changes fastest.
Arguments:
- inputs: bfloat16 [6, 32, 16384], replicated, may hold values from -4 to 4
- in_blocks: bfloat16 [4, 128, 4, 8, 128, 128], P('pipe', 'width'), may hold values from -0.1875 to 0.1875
- rec_blocks: bfloat16 [4, 128, 4, 8, 128, 128], P('pipe', 'width'), may hold values from -0.1875 to 0.1875
- in_cols: int32 [4, 128, 4, 8], P('pipe', 'width'), may hold values from 0 to 127, as said below
- rec_cols: int32 [4, 128, 4, 8], P('pipe', 'width'), may hold values from 0 to 127, as said below
- bias: float32 [4, 4, 16384], P('pipe', None, 'width'), may hold values from -1 to 1
Outputs:
- hidden_seq: bfloat16 [4, 6, 32, 16384], P('pipe', None, None, 'width')
- cells: float32 [4, 32, 16384], P('pipe', None, 'width')
The draws below stay inside these ranges and needn't reach their ends.
Inputs may be any that keep to these rules, and one draw needn't show every extreme that they name: Each in_cols[l, j, g] holds 8 different hidden block numbers. Each rec_cols[l, j, g] holds 8 different hidden block numbers.
All inputs are finite; a program needn't handle non-finite values.
Results may differ from the reference program's by a relative error of at most 0.0033.
Values may be sent and summed in bfloat16 or wider, within the bound.
No kernel may reach another device: no remote copies, remote signals or barrier semaphores. Data moves between devices by JAX's collectives and lax.ppermute only.
A program may use at most 64 MiB of HBM per device.

```python
import jax
import jax.numpy as jnp
from jax import lax

H = 16384
BS = 128
HB = 128
KB = 8
B = 32
STEPS = 6
LAYERS = 4


def pick_blocks(key):
    scores = jax.random.randint(key, (LAYERS, HB, 4, HB), 0, 65536, dtype=jnp.int32)
    scores = scores * HB + jnp.arange(HB, dtype=jnp.int32)
    values_top, chosen = lax.top_k(scores, KB)
    return chosen.astype(jnp.int32)


def draw_in_cols(key, part):
    key = jax.random.fold_in(key, 11)
    return pick_blocks(key)


def draw_rec_cols(key, part):
    key = jax.random.fold_in(key, 12)
    return pick_blocks(key)


def block_levels(rng, dims, shards, smallest, largest):
    loudness = 1.0
    for axis_at, parts in shards:
        draws = jax.random.uniform(jax.random.fold_in(jax.random.fold_in(rng, 6), axis_at), (parts,), jnp.float32, smallest / len(shards), largest / len(shards))
        loudness = loudness * jnp.repeat(jnp.exp(draws), dims[axis_at] // parts).reshape((-1,) + (1,) * (len(dims) - 1 - axis_at))
    return loudness


def bell_draw(own_key, extent, scale, reach, shards=(), held_as=jnp.bfloat16):
    entries = scale * jax.random.normal(own_key, extent, jnp.float32)
    if shards:
        entries = entries * block_levels(own_key, extent, shards, -0.22, 0.18)
    return jnp.clip(entries, -reach, reach).astype(held_as)


def setup_inputs(seed: int = 0) -> dict:
    key_of = jax.random.split(jax.random.key(seed), 7)
    return {
        "inputs": bell_draw(key_of[0], (STEPS, B, H), 1.0, 4.0),
        "in_blocks": bell_draw(key_of[1], (LAYERS, HB, 4, KB, BS, BS), (KB * BS) ** -0.5, 0.1875, ((0, 4), (1, 32))),
        "rec_blocks": bell_draw(key_of[2], (LAYERS, HB, 4, KB, BS, BS), (KB * BS) ** -0.5, 0.1875, ((0, 4), (1, 32))),
        "in_cols": draw_in_cols(jax.random.fold_in(key_of[6], 71), 0),
        "rec_cols": draw_rec_cols(jax.random.fold_in(key_of[6], 71), 0),
        "bias": jnp.clip(jax.random.uniform(key_of[5], (LAYERS, 4, H), jnp.float32, -1.0, 1.0) * block_levels(key_of[5], (LAYERS, 4, H), ((0, 4), (2, 32)), -0.4, 0.0), -1.0, 1.0),
    }


def reference(inputs, in_blocks, rec_blocks, in_cols, rec_cols, bias):
    lower_seq = inputs
    sequences = []
    cell_rows = []
    for layer_index in range(LAYERS):
        weights = jnp.concatenate([in_blocks[layer_index], rec_blocks[layer_index]], axis=2).astype(jnp.float32)
        block_index = jnp.concatenate([in_cols[layer_index], rec_cols[layer_index] + HB], axis=2).reshape(-1)
        offsets = bias[layer_index].reshape(4, HB, BS).transpose(1, 0, 2)
        hidden_state = jnp.zeros((B, H), jnp.bfloat16)
        cell_state = jnp.zeros((B, H), jnp.float32)
        outputs = []
        for step_index in range(STEPS):
            stacked = jnp.concatenate([lower_seq[step_index], hidden_state], axis=1).reshape(B, 2 * HB, BS)
            picked = jnp.take(stacked, block_index, axis=1).reshape(B, HB, 4, 2 * KB, BS).astype(jnp.float32)
            gate_sums = jnp.einsum("rjgka,jgkab->rjgb", picked, weights) + offsets
            input_gate = jax.nn.sigmoid(gate_sums[:, :, 0]).reshape(B, H)
            forget_gate = jax.nn.sigmoid(gate_sums[:, :, 1]).reshape(B, H)
            cell_input = jnp.tanh(gate_sums[:, :, 2]).reshape(B, H)
            output_gate = jax.nn.sigmoid(gate_sums[:, :, 3]).reshape(B, H)
            cell_state = forget_gate * cell_state + input_gate * cell_input
            hidden_state = (output_gate * jnp.tanh(cell_state)).astype(jnp.bfloat16)
            outputs.append(hidden_state)
        lower_seq = jnp.stack(outputs)
        sequences.append(lower_seq)
        cell_rows.append(cell_state)
    return jnp.stack(sequences), jnp.stack(cell_rows)
```

```python
import functools

import jax
import jax.numpy as jnp
from jax import lax
from jax.experimental import pallas as pl
from jax.experimental.pallas import tpu as pltpu
from jax.sharding import Mesh
from jax.sharding import PartitionSpec as P

LAG = 2
F32 = jnp.float32
BF16 = jnp.bfloat16
WIDTH = ("y", "x", "core")


def row_sums(index_ref, x_ref, w_ref, row):
    blocks = w_ref.shape[1]
    edge = w_ref.shape[2]
    picked = jnp.concatenate([x_ref[index_ref[row * blocks + k]] for k in range(blocks)], axis=1)
    return jnp.dot(picked, w_ref[row].reshape(blocks * edge, edge), preferred_element_type=F32)


def input_kernel(index_ref, x_ref, w_ref, bias_ref, out_ref):
    for row in range(w_ref.shape[0]):
        out_ref[row] = row_sums(index_ref, x_ref, w_ref, row) + bias_ref[row]


def state_kernel(step_count, index_ref, step_ref, h_ref, w_ref, partial_ref, cell_ref, cell_out, rows_out, send_out):
    step = step_ref[0]
    started = step >= 0
    running = started & (step < step_count)
    edge = h_ref.shape[2]
    for j in range(cell_ref.shape[0]):
        sums = [
            partial_ref[4 * j + g] + row_sums(index_ref, h_ref, w_ref, 4 * j + g) for g in range(4)
        ]
        before = cell_ref[j]
        cell = jax.nn.sigmoid(sums[1]) * before + jax.nn.sigmoid(sums[0]) * jnp.tanh(sums[2])
        output = jax.nn.sigmoid(sums[3]) * jnp.tanh(cell)
        output = jnp.where(started, output, 0.0).astype(BF16)
        cell_out[j] = jnp.where(running, cell, before)
        rows_out[:, j * edge:(j + 1) * edge] = output
        for peer in range(send_out.shape[0]):
            send_out[peer, j] = output


def vmem():
    return pl.BlockSpec(memory_space=pltpu.VMEM)


def smem():
    return pl.BlockSpec(memory_space=pltpu.SMEM)


def input_sums(index, x, w, bias):
    rows = w.shape[0]
    return pl.pallas_call(
        input_kernel,
        out_shape=jax.ShapeDtypeStruct((rows, x.shape[1], x.shape[2]), F32),
        in_specs=[smem(), vmem(), vmem(), vmem()],
        out_specs=vmem(),
        compiler_params=pltpu.CompilerParams(vmem_limit_bytes=24 * 2**20),
        cost_estimate=pl.CostEstimate(flops=2 * w.size * 32, bytes_accessed=2 * w.size, transcendentals=0),
        name="input_sums",
    )(index, x, w, bias)


def state_step(index, step, h, w, partial, cell, step_count, peers):
    per_device, row_count, edge = cell.shape
    return pl.pallas_call(
        functools.partial(state_kernel, step_count),
        out_shape=(
            jax.ShapeDtypeStruct(cell.shape, F32),
            jax.ShapeDtypeStruct((row_count, per_device * edge), BF16),
            jax.ShapeDtypeStruct((peers, per_device, row_count, edge), BF16),
        ),
        in_specs=[smem(), smem(), vmem(), vmem(), vmem(), vmem()],
        out_specs=(vmem(), vmem(), vmem()),
        compiler_params=pltpu.CompilerParams(vmem_limit_bytes=24 * 2**20),
        cost_estimate=pl.CostEstimate(flops=2 * w.size * 32, bytes_accessed=2 * w.size, transcendentals=0),
        name="state_step",
    )(index, step, h, w, partial, cell)


def other_core(x):
    return lax.ppermute(x, "core", [(0, 1), (1, 0)])


def body(inputs, in_blocks, rec_blocks, in_cols, rec_cols, bias):
    layer = lax.axis_index("pipe")
    layers = lax.axis_size("pipe")
    core = lax.axis_index("core")
    chips = lax.axis_size("y") * lax.axis_size("x")
    step_count, row_count, hidden = inputs.shape
    _, per_device, gates, kept, edge, _ = in_blocks.shape
    total = hidden // edge
    half = total // 2
    rows = per_device * gates
    w_in = in_blocks.reshape(rows, kept, edge, edge)
    w_rec = rec_blocks.reshape(rows, kept, edge, edge)

    def place(cols):
        device = cols // per_device
        return ((device % 2) ^ core) * half + (device // 2) * per_device + cols % per_device

    in_flat = in_cols.reshape(-1)
    in_index = jnp.where(layer == 0, in_flat, place(in_flat))
    rec_index = place(rec_cols.reshape(-1))
    offsets = bias[0].reshape(gates, per_device, edge).transpose(1, 0, 2).reshape(rows, 1, edge)
    offsets = jnp.broadcast_to(offsets, (rows, 8, edge))[:, :1]

    tick_count = step_count + LAG * (layers - 1)
    up = [(i, i + 1) for i in range(layers - 1)]
    state = jnp.zeros((total, row_count, edge), BF16)
    cell = jnp.zeros((per_device, row_count, edge), F32)
    arrived = {}
    outputs = []
    for tick in range(tick_count):
        fresh = None
        if tick < step_count:
            fresh = inputs[tick].reshape(row_count, total, edge).transpose(1, 0, 2)
        if tick >= LAG:
            lower = arrived[tick - LAG]
            lower = jnp.concatenate([lower, other_core(lower)], axis=0)
            x = lower if fresh is None else jnp.where(layer == 0, fresh, lower)
        else:
            x = fresh
        partial = input_sums(in_index, x, w_in, offsets)
        step = (tick - LAG * layer).astype(jnp.int32).reshape(1)
        cell, out_rows, send = state_step(rec_index, step, state, w_rec, partial, cell, step_count, chips)
        outputs.append(out_rows)
        if tick < tick_count - 1:
            mine = lax.all_to_all(send, ("y", "x"), 0, 0).reshape(half, row_count, edge)
            if tick < tick_count - LAG:
                arrived[tick] = lax.ppermute(mine, "pipe", up)
            state = jnp.concatenate([mine, other_core(mine)], axis=0)
    sequence = lax.dynamic_slice_in_dim(jnp.stack(outputs), LAG * layer, step_count, 0)
    cells = cell.transpose(1, 0, 2).reshape(row_count, per_device * edge)
    return sequence[None], cells[None]


def solution(mesh):
    layers, width = mesh.devices.shape
    grid = Mesh(mesh.devices.reshape(layers, 4, width // 8, 2), ("pipe",) + WIDTH)
    return jax.shard_map(
        body,
        mesh=grid,
        in_specs=(
            P(),
            P("pipe", WIDTH, None, None, None, None),
            P("pipe", WIDTH, None, None, None, None),
            P("pipe", WIDTH, None, None),
            P("pipe", WIDTH, None, None),
            P("pipe", None, WIDTH),
        ),
        out_specs=(P("pipe", None, None, WIDTH), P("pipe", None, WIDTH)),
        check_vma=False,
    )
```

```python
import functools

import jax
import jax.numpy as jnp
from jax import lax
from jax.experimental import pallas as pl
from jax.experimental.pallas import tpu as pltpu
from jax.sharding import Mesh
from jax.sharding import PartitionSpec as P

LAG = 2
F32 = jnp.float32
BF16 = jnp.bfloat16
WIDTH = ("y", "x", "core")
MIB = 2**20


def vmem():
    return pl.BlockSpec(memory_space=pltpu.VMEM)


def smem():
    return pl.BlockSpec(memory_space=pltpu.SMEM)


def held(x):
    return pltpu.with_memory_space_constraint(x, pltpu.VMEM)


def hbm():
    return pl.BlockSpec(memory_space=pltpu.HBM)


def unmoved(x):
    return pltpu.with_memory_space_constraint(x, pltpu.HBM)


def load_kernel(w_ref, out_ref):
    pltpu.sync_copy(w_ref, out_ref)


def load(w):
    return pl.pallas_call(
        load_kernel,
        out_shape=pltpu.VMEM(w.shape, w.dtype),
        in_specs=[hbm()],
        out_specs=vmem(),
        compiler_params=pltpu.CompilerParams(vmem_limit_bytes=2 * MIB),
        name="load_weights",
    )(unmoved(w))


def row_sums(pick, index_ref, w_ref, row):
    blocks = w_ref.shape[1]
    edge = w_ref.shape[2]
    picked = jnp.concatenate([pick(index_ref[row * blocks + k]) for k in range(blocks)], axis=1)
    return jnp.dot(picked, w_ref[row].reshape(blocks * edge, edge), preferred_element_type=F32)


def from_halves(mine_ref, other_ref):
    half = mine_ref.shape[0]

    def pick(i):
        return jnp.where(
            i < half, mine_ref[jnp.minimum(i, half - 1)], other_ref[jnp.maximum(i - half, 0)]
        )

    return pick


def from_rows(rows_ref, edge):
    return lambda i: rows_ref[:, pl.ds(pl.multiple_of(i * edge, edge), edge)]


def input_kernel(tick, step_count, layer_ref, index_ref, inputs_ref, mine_ref, other_ref, w_ref, bias_ref, out_ref, *scratch):
    edge = w_ref.shape[2]
    row_count = out_ref.shape[1]

    def fill(pick):
        for row in range(w_ref.shape[0]):
            bias = jnp.broadcast_to(bias_ref[row], (row_count, edge))
            out_ref[row] = row_sums(pick, index_ref, w_ref, row) + bias

    if tick >= step_count:
        fill(from_halves(mine_ref, other_ref))
        return
    fresh_ref, arrived = scratch

    @pl.when(layer_ref[0] == 0)
    def _():
        pltpu.make_async_copy(inputs_ref.at[tick], fresh_ref, arrived).start()
        pltpu.make_async_copy(inputs_ref.at[tick], fresh_ref, arrived).wait()
        fill(from_rows(fresh_ref, edge))

    @pl.when(layer_ref[0] != 0)
    def _():
        if mine_ref is None:
            out_ref[...] = jnp.zeros_like(out_ref)
        else:
            fill(from_halves(mine_ref, other_ref))


def without_lower(kernel):
    def run(layer_ref, index_ref, inputs_ref, *rest):
        kernel(layer_ref, index_ref, inputs_ref, None, None, *rest)

    return run


def input_sums(tick, layer, index, inputs, lower, w, bias):
    step_count, row_count, hidden = inputs.shape
    rows = w.shape[0]
    kernel = functools.partial(input_kernel, tick, step_count)
    return pl.pallas_call(
        kernel if lower else without_lower(kernel),
        out_shape=pltpu.VMEM((rows, row_count, w.shape[3]), F32),
        in_specs=[smem(), smem(), hbm()] + [vmem()] * (len(lower) + 2),
        out_specs=vmem(),
        scratch_shapes=[pltpu.VMEM((row_count, hidden), BF16), pltpu.SemaphoreType.DMA] if tick < step_count else [],
        compiler_params=pltpu.CompilerParams(vmem_limit_bytes=8 * MIB),
        cost_estimate=pl.CostEstimate(flops=2 * w.size * 32, bytes_accessed=w.size, transcendentals=0),
        name="input_sums",
    )(layer, index, unmoved(inputs), *[held(part) for part in lower], w, held(bias))


def gates_to_state(sums, before, started, running):
    cell = jax.nn.sigmoid(sums[1]) * before + jax.nn.sigmoid(sums[0]) * jnp.tanh(sums[2])
    output = jax.nn.sigmoid(sums[3]) * jnp.tanh(cell)
    output = jnp.where(started, output, 0.0).astype(BF16)
    return jnp.where(running, cell, before), output


def put(j, output, rows_out, send_out):
    edge = output.shape[1]
    rows_out[:, j * edge:(j + 1) * edge] = output
    for peer in range(send_out.shape[0]):
        send_out[peer, j] = output


def first_kernel(layer_ref, index_ref, inputs_ref, w_hbm, bias_ref, cell_out, rows_out, send_out, w_out, fresh_ref, arrived, loaded):
    per_device, row_count, edge = cell_out.shape
    fresh = pltpu.make_async_copy(inputs_ref.at[0], fresh_ref, arrived)
    fresh.start()
    loads = [
        pltpu.make_async_copy(w_hbm.at[pl.ds(4 * j, 4)], w_out.at[pl.ds(4 * j, 4)], loaded.at[j])
        for j in range(per_device)
    ]
    for copy in loads:
        copy.start()
    fresh.wait()
    started = layer_ref[0] == 0
    pick = from_rows(fresh_ref, edge)
    for j in range(per_device):
        loads[j].wait()
        sums = [
            row_sums(pick, index_ref, w_out, 4 * j + g) + jnp.broadcast_to(bias_ref[4 * j + g], (row_count, edge))
            for g in range(4)
        ]
        cell_out[j], output = gates_to_state(sums, jnp.zeros((row_count, edge), F32), started, started)
        put(j, output, rows_out, send_out)


def first_step(layer, index, inputs, w, bias, per_device, peers):
    _, row_count, hidden = inputs.shape
    rows, _, edge, _ = w.shape
    return pl.pallas_call(
        first_kernel,
        out_shape=(
            pltpu.VMEM((per_device, row_count, edge), F32),
            jax.ShapeDtypeStruct((row_count, per_device * edge), BF16),
            pltpu.VMEM((peers, per_device, row_count, edge), BF16),
            pltpu.VMEM(w.shape, w.dtype),
        ),
        in_specs=[smem(), smem(), hbm(), hbm(), vmem()],
        out_specs=(vmem(), vmem(), vmem(), vmem()),
        scratch_shapes=[
            pltpu.VMEM((row_count, hidden), BF16),
            pltpu.SemaphoreType.DMA,
            pltpu.SemaphoreType.DMA((per_device,)),
        ],
        compiler_params=pltpu.CompilerParams(vmem_limit_bytes=8 * MIB),
        name="first_step",
    )(layer, index, unmoved(inputs), unmoved(w), held(bias))


def state_kernel(step_count, step_ref, index_ref, mine_ref, other_ref, w_ref, partial_ref, cell_ref, cell_out, rows_out, send_out):
    step = step_ref[0]
    started = step >= 0
    running = started & (step < step_count)
    pick = from_halves(mine_ref, other_ref)
    for j in range(cell_ref.shape[0]):
        sums = [partial_ref[4 * j + g] + row_sums(pick, index_ref, w_ref, 4 * j + g) for g in range(4)]
        cell_out[j], output = gates_to_state(sums, cell_ref[j], started, running)
        put(j, output, rows_out, send_out)


def state_step(step, index, state, w, partial, cell, step_count, peers):
    per_device, row_count, edge = cell.shape
    return pl.pallas_call(
        functools.partial(state_kernel, step_count),
        out_shape=(
            pltpu.VMEM(cell.shape, F32),
            jax.ShapeDtypeStruct((row_count, per_device * edge), BF16),
            pltpu.VMEM((peers, per_device, row_count, edge), BF16),
        ),
        in_specs=[smem(), smem()] + [vmem()] * 5,
        out_specs=(vmem(), vmem(), vmem()),
        compiler_params=pltpu.CompilerParams(vmem_limit_bytes=8 * MIB),
        cost_estimate=pl.CostEstimate(flops=2 * w.size * 32, bytes_accessed=w.size, transcendentals=0),
        name="state_step",
    )(step, index, *[held(part) for part in state], w, partial, cell)


def other_core(x):
    return lax.ppermute(x, "core", [(0, 1), (1, 0)])


def body(inputs, in_blocks, rec_blocks, in_cols, rec_cols, bias):
    layer = lax.axis_index("pipe")
    layers = lax.axis_size("pipe")
    core = lax.axis_index("core")
    chips = lax.axis_size("y") * lax.axis_size("x")
    step_count, row_count, hidden = inputs.shape
    _, per_device, gates, kept, edge, _ = in_blocks.shape
    total = hidden // edge
    half = total // 2
    rows = per_device * gates

    def place(cols):
        device = cols // per_device
        return ((device % 2) ^ core) * half + (device // 2) * per_device + cols % per_device

    in_flat = in_cols.reshape(-1)
    in_index = jnp.where(layer == 0, in_flat, place(in_flat))
    rec_index = place(rec_cols.reshape(-1))
    offsets = bias[0].reshape(gates, per_device, edge).transpose(1, 0, 2).reshape(rows, 1, edge)
    layer_ref = layer.astype(jnp.int32).reshape(1)
    w_in = in_blocks.reshape(rows, kept, edge, edge)
    w_rec = rec_blocks.reshape(rows, kept, edge, edge)

    tick_count = step_count + LAG * (layers - 1)
    up = [(i, i + 1) for i in range(layers - 1)]
    cell, out_rows, send, w_in = first_step(layer_ref, in_index, inputs, w_in, offsets, per_device, chips)
    send, w_rec = lax.optimization_barrier((send, w_rec))
    w_rec = load(w_rec)
    arrived = {}
    outputs = [out_rows]
    for tick in range(1, tick_count):
        mine = lax.all_to_all(send, ("y", "x"), 0, 0).reshape(half, row_count, edge)
        lower = ()
        if tick >= LAG:
            low, _ = lax.optimization_barrier((arrived[tick - LAG], out_rows))
            lower = (low, other_core(low))
        partial = input_sums(tick, layer_ref, in_index, inputs, lower, w_in, offsets)
        mine, partial = lax.optimization_barrier((mine, partial))
        if tick <= tick_count - LAG:
            arrived[tick - 1] = lax.ppermute(mine, "pipe", up)
        state = (mine, other_core(mine))
        step = (tick - LAG * layer).astype(jnp.int32).reshape(1)
        cell, out_rows, send = state_step(step, rec_index, state, w_rec, partial, cell, step_count, chips)
        outputs.append(out_rows)
    sequence = lax.dynamic_slice_in_dim(jnp.stack(outputs), LAG * layer, step_count, 0)
    cells = cell.transpose(1, 0, 2).reshape(row_count, per_device * edge)
    return sequence[None], cells[None]


def solution(mesh):
    layers, width = mesh.devices.shape
    grid = Mesh(mesh.devices.reshape(layers, 4, width // 8, 2), ("pipe",) + WIDTH)
    return jax.shard_map(
        body,
        mesh=grid,
        in_specs=(
            P(),
            P("pipe", WIDTH, None, None, None, None),
            P("pipe", WIDTH, None, None, None, None),
            P("pipe", WIDTH, None, None),
            P("pipe", WIDTH, None, None),
            P("pipe", None, WIDTH),
        ),
        out_specs=(P("pipe", None, None, WIDTH), P("pipe", None, WIDTH)),
        check_vma=False,
    )
```

```python
import functools
import math

import jax
import jax.numpy as jnp
from jax import lax
from jax.experimental import pallas as pl
from jax.experimental.pallas import tpu as pltpu
from jax.sharding import Mesh
from jax.sharding import PartitionSpec as P

LAG = 2
F32 = jnp.float32
BF16 = jnp.bfloat16
WIDTH = ("y", "x", "core")
MIB = 2**20


def vmem():
    return pl.BlockSpec(memory_space=pltpu.VMEM)


def smem():
    return pl.BlockSpec(memory_space=pltpu.SMEM)


def held(x):
    return pltpu.with_memory_space_constraint(x, pltpu.VMEM)


def hbm():
    return pl.BlockSpec(memory_space=pltpu.HBM)


def unmoved(x):
    return pltpu.with_memory_space_constraint(x, pltpu.HBM)


def group(ref, j, size):
    return ref.at[pl.ds(size * j, size)]


def stream(w_hbm, w_ref, loaded):
    groups = loaded.shape[0]
    size = w_ref.shape[0] // groups
    copies = [
        pltpu.make_async_copy(group(w_hbm, j, size), group(w_ref, j, size), loaded.at[j])
        for j in range(groups)
    ]
    for copy in copies:
        copy.start()
    return copies


def load_kernel(w_ref, after_ref, out_ref, loaded):
    for copy in stream(w_ref, out_ref, loaded):
        copy.wait()


def load(w, after):
    return pl.pallas_call(
        load_kernel,
        out_shape=pltpu.VMEM(w.shape, w.dtype),
        in_specs=[hbm(), pl.BlockSpec(memory_space=pl.ANY)],
        out_specs=vmem(),
        scratch_shapes=[pltpu.SemaphoreType.DMA((8,))],
        compiler_params=pltpu.CompilerParams(vmem_limit_bytes=8 * MIB),
        cost_estimate=pl.CostEstimate(flops=0, bytes_accessed=2 * w.size, transcendentals=0),
        name="load_weights",
    )(unmoved(w), after)


def row_sums(pick, index_ref, w_ref, row):
    blocks = w_ref.shape[1]
    edge = w_ref.shape[2]
    picked = jnp.concatenate([pick(index_ref[row * blocks + k]) for k in range(blocks)], axis=1)
    return jnp.dot(picked, w_ref[row].reshape(blocks * edge, edge), preferred_element_type=F32)


def from_halves(mine_ref, other_ref):
    half = mine_ref.shape[0]

    def pick(i):
        return jnp.where(
            i < half, mine_ref[jnp.minimum(i, half - 1)], other_ref[jnp.maximum(i - half, 0)]
        )

    return pick


def from_rows(rows_ref, edge):
    return lambda i: rows_ref[:, pl.ds(pl.multiple_of(i * edge, edge), edge)]


def input_kernel(tick, step_count, *refs):
    layer_ref, index_ref = refs[:2]
    fresh_ref = refs[2] if tick < step_count else None
    lower_refs = refs[-5:-3] if tick >= LAG else None
    w_ref, bias_ref, out_ref = refs[-3:]
    edge = w_ref.shape[2]
    row_count = out_ref.shape[1]

    def fill(pick):
        for row in range(w_ref.shape[0]):
            bias = jnp.broadcast_to(bias_ref[row], (row_count, edge))
            out_ref[row] = row_sums(pick, index_ref, w_ref, row) + bias

    step = tick - LAG * layer_ref[0]
    if fresh_ref is not None:
        @pl.when(layer_ref[0] == 0)
        def _():
            fill(from_rows(fresh_ref, edge))

    if lower_refs is not None:
        @pl.when((layer_ref[0] != 0) & (step >= 0) & (step < step_count))
        def _():
            fill(from_halves(*lower_refs))


def input_sums(tick, layer, index, fresh, lower, w, bias, step_count):
    rows = w.shape[0]
    x = [held(part) for part in ((fresh,) if tick < step_count else ()) + lower]
    row_count = (fresh if fresh is not None else lower[0]).shape[-2]
    return pl.pallas_call(
        functools.partial(input_kernel, tick, step_count),
        out_shape=pltpu.VMEM((rows, row_count, w.shape[3]), F32),
        in_specs=[smem(), smem()] + [vmem()] * (len(x) + 2),
        out_specs=vmem(),
        compiler_params=pltpu.CompilerParams(vmem_limit_bytes=8 * MIB),
        cost_estimate=pl.CostEstimate(flops=2 * w.size * 32, bytes_accessed=w.size, transcendentals=0),
        name="input_sums",
    )(layer, index, *x, held(w), held(bias))


def gates_to_state(sums, before):
    cell = jax.nn.sigmoid(sums[1]) * before + jax.nn.sigmoid(sums[0]) * jnp.tanh(sums[2])
    output = jax.nn.sigmoid(sums[3]) * jnp.tanh(cell)
    return cell, output.astype(BF16)


class Sender:
    def __init__(self, send_out, spread_ref, sent):
        self.send_out, self.spread_ref, self.sent = send_out, spread_ref, sent
        self.copies = []

    def put(self, j, output):
        for peer in range(self.spread_ref.shape[1]):
            self.spread_ref[j, peer] = output
        copy = pltpu.make_async_copy(self.spread_ref.at[j], self.send_out.at[:, j], self.sent.at[j])
        copy.start()
        self.copies.append(copy)

    def finish(self):
        for copy in self.copies:
            copy.wait()


def send_scratch(cell_shape, peers):
    per_device, row_count, edge = cell_shape
    return [pltpu.VMEM((per_device, peers, row_count, edge), BF16), pltpu.SemaphoreType.DMA((per_device,))]


def state_out(cell_shape, peers):
    per_device, row_count, edge = cell_shape
    return (
        pltpu.VMEM(cell_shape, F32),
        jax.ShapeDtypeStruct((row_count, per_device * edge), BF16),
        pltpu.HBM((peers, *cell_shape), BF16),
    )


def first_kernel(layer_ref, index_ref, inputs_ref, w_hbm, bias_ref, cell_out, rows_out, send_out, next_out, fresh_ref, w_out, arrived, loaded, spread_ref, sent):
    per_device, row_count, edge = cell_out.shape
    fresh = pltpu.make_async_copy(inputs_ref.at[0], fresh_ref, arrived.at[0])
    later = pltpu.make_async_copy(inputs_ref.at[1], next_out, arrived.at[1])
    fresh.start()
    copies = stream(w_hbm, w_out, loaded)
    later.start()

    @pl.when(layer_ref[0] == 0)
    def _():
        fresh.wait()
        sender = Sender(send_out, spread_ref, sent)
        pick = from_rows(fresh_ref, edge)
        for j, copy in enumerate(copies):
            copy.wait()
            sums = [
                row_sums(pick, index_ref, w_out, 4 * j + g) + jnp.broadcast_to(bias_ref[4 * j + g], (row_count, edge))
                for g in range(4)
            ]
            cell_out[j], output = gates_to_state(sums, jnp.zeros((row_count, edge), F32))
            rows_out[:, j * edge:(j + 1) * edge] = output
            sender.put(j, output)
        sender.finish()

    @pl.when(layer_ref[0] != 0)
    def _():
        idle = Sender(send_out, spread_ref, sent)
        for j in range(per_device):
            idle.put(j, jnp.zeros((row_count, edge), BF16))
        for ref in (cell_out, rows_out):
            ref[...] = jnp.zeros_like(ref)
        idle.finish()
        fresh.wait()
        for copy in copies:
            copy.wait()

    later.wait()


def first_step(layer, index, inputs, w, bias, per_device, peers):
    _, row_count, hidden = inputs.shape
    edge = w.shape[2]
    return pl.pallas_call(
        first_kernel,
        out_shape=state_out((per_device, row_count, edge), peers)
        + (pltpu.VMEM((row_count, hidden), BF16),),
        in_specs=[smem(), smem(), hbm(), hbm(), vmem()],
        out_specs=(vmem(), vmem(), hbm(), vmem()),
        scratch_shapes=[
            pltpu.VMEM((row_count, hidden), BF16),
            pltpu.VMEM(w.shape, w.dtype),
            pltpu.SemaphoreType.DMA((2,)),
            pltpu.SemaphoreType.DMA((per_device,)),
            *send_scratch((per_device, row_count, edge), peers),
        ],
        compiler_params=pltpu.CompilerParams(vmem_limit_bytes=12 * MIB),
        name="first_step",
    )(layer, index, unmoved(inputs), unmoved(w), held(bias))


def state_kernel(tick, step_count, layer_ref, index_ref, inputs_ref, mine_ref, other_ref, w_ref, partial_ref, cell_ref, cell_out, rows_out, send_out, *rest):
    *fetch, spread_ref, sent = rest
    step = tick - LAG * layer_ref[0]
    active = (step >= 0) & (step < step_count)
    edge = cell_ref.shape[2]
    is_first = layer_ref[0] == 0
    if fetch:
        next_out, arrived = fetch
        later = pltpu.make_async_copy(inputs_ref.at[tick + 1], next_out, arrived)
        pl.when(is_first)(later.start)

    @pl.when(active)
    def _():
        pick = from_halves(mine_ref, other_ref)
        sender = Sender(send_out, spread_ref, sent)
        for j in range(cell_ref.shape[0]):
            sums = [partial_ref[4 * j + g] + row_sums(pick, index_ref, w_ref, 4 * j + g) for g in range(4)]
            cell_out[j], output = gates_to_state(sums, cell_ref[j])
            rows_out[:, j * edge:(j + 1) * edge] = output
            sender.put(j, output)
        sender.finish()

    @pl.when(jnp.logical_not(active))
    def _():
        idle = Sender(send_out, spread_ref, sent)
        for j in range(cell_ref.shape[0]):
            idle.put(j, jnp.zeros(cell_ref.shape[1:], BF16))
        cell_out[...] = cell_ref[...]
        rows_out[...] = jnp.zeros_like(rows_out)
        idle.finish()

    if fetch:
        pl.when(is_first)(later.wait)


def state_step(tick, layer, index, state, w, partial, cell, inputs, peers):
    step_count, row_count, hidden = inputs.shape
    fetch = tick + 1 < step_count
    outs = pl.pallas_call(
        functools.partial(state_kernel, tick, step_count),
        out_shape=state_out(cell.shape, peers) + ((pltpu.VMEM((row_count, hidden), BF16),) if fetch else ()),
        in_specs=[smem(), smem(), hbm()] + [vmem()] * 5,
        out_specs=(vmem(), vmem(), hbm()) + (vmem(),) * fetch,
        scratch_shapes=[pltpu.SemaphoreType.DMA] * fetch + send_scratch(cell.shape, peers),
        compiler_params=pltpu.CompilerParams(vmem_limit_bytes=8 * MIB),
        cost_estimate=pl.CostEstimate(flops=2 * w.size * 32, bytes_accessed=w.size, transcendentals=0),
        name="state_step",
    )(layer, index, unmoved(inputs), *[held(part) for part in state], held(w), partial, cell)
    return outs if fetch else (*outs, None)


def exchange(x, target):
    sizes = [lax.axis_size(axis) for axis in ("pipe",) + WIDTH]
    route = []
    for source in range(math.prod(sizes)):
        place, rest = [], source
        for size in reversed(sizes):
            place.insert(0, rest % size)
            rest //= size
        to = 0
        for size, at in zip(sizes, target(*place)):
            to = to * size + at % size
        route.append((source, to))
    return lax.ppermute(x, ("pipe",) + WIDTH, route)


def other_core(x):
    return exchange(x, lambda layer, y, x_at, core: (layer, y, x_at, 1 - core))


def upward(x):
    return exchange(x, lambda layer, y, x_at, core: (layer + 1, y, x_at, core))


def body(inputs, in_blocks, rec_blocks, in_cols, rec_cols, bias):
    layer = lax.axis_index("pipe")
    layers = lax.axis_size("pipe")
    core = lax.axis_index("core")
    step_count, row_count, hidden = inputs.shape
    _, per_device, gates, kept, edge, _ = in_blocks.shape
    total = hidden // edge
    half = total // 2
    rows = per_device * gates

    chips = lax.axis_size("y") * lax.axis_size("x")

    def place(cols):
        device = cols // per_device
        return ((device % 2) ^ core) * half + (device // 2) * per_device + cols % per_device

    in_flat = in_cols.reshape(-1)
    in_index = jnp.where(layer == 0, in_flat, place(in_flat))
    rec_index = place(rec_cols.reshape(-1))
    offsets = bias[0].reshape(gates, per_device, edge).transpose(1, 0, 2).reshape(rows, 1, edge)
    layer_ref = layer.astype(jnp.int32).reshape(1)
    w_in = in_blocks.reshape(rows, kept, edge, edge)
    w_rec = rec_blocks.reshape(rows, kept, edge, edge)

    tick_count = step_count + LAG * (layers - 1)
    steps = [tick - LAG * layer for tick in range(tick_count)]
    fed = [(layer > 0) & (step >= 0) & (step < step_count) for step in steps]
    layer_ref, fed, in_index, rec_index = lax.optimization_barrier((layer_ref, fed, in_index, rec_index))
    cell, out_rows, send, fresh = first_step(layer_ref, in_index, inputs, w_in, offsets, per_device, chips)
    arrived = {}
    outputs = [out_rows]
    for tick in range(1, tick_count):
        mine = lax.all_to_all(send, ("y", "x"), 0, 0).reshape(half, row_count, edge)
        lower = ()
        if tick >= LAG:
            low = arrived[tick - LAG]
            lower = (low, lax.cond(fed[tick], other_core, jnp.zeros_like, low))
        partial = input_sums(tick, layer_ref, in_index, fresh, lower, w_in, offsets, step_count)
        mine, partial = lax.optimization_barrier((mine, partial))
        other = other_core(mine)
        if tick <= tick_count - LAG:
            arrived[tick - 1] = upward(mine)
        state = (mine, other)
        cell, out_rows, send, fresh = state_step(tick, layer_ref, rec_index, state, load(w_rec, mine), partial, cell, inputs, chips)
        outputs.append(out_rows)
    sequence = lax.dynamic_slice_in_dim(jnp.stack(outputs), LAG * layer, step_count, 0)
    cells = cell.transpose(1, 0, 2).reshape(row_count, per_device * edge)
    return sequence[None], cells[None]


def solution(mesh):
    layers, width = mesh.devices.shape
    grid = Mesh(mesh.devices.reshape(layers, 4, width // 8, 2), ("pipe",) + WIDTH)
    return jax.shard_map(
        body,
        mesh=grid,
        in_specs=(
            P(),
            P("pipe", WIDTH, None, None, None, None),
            P("pipe", WIDTH, None, None, None, None),
            P("pipe", WIDTH, None, None),
            P("pipe", WIDTH, None, None),
            P("pipe", None, WIDTH),
        ),
        out_specs=(P("pipe", None, None, WIDTH), P("pipe", None, WIDTH)),
        check_vma=False,
    )
```

```python
import functools
import math

import jax
import jax.numpy as jnp
from jax import lax
from jax.experimental import pallas as pl
from jax.experimental.pallas import tpu as pltpu
from jax.sharding import Mesh
from jax.sharding import PartitionSpec as P

LAG = 2
F32 = jnp.float32
BF16 = jnp.bfloat16
WIDTH = ("y", "x", "core")
MIB = 2**20


def vmem():
    return pl.BlockSpec(memory_space=pltpu.VMEM)


def smem():
    return pl.BlockSpec(memory_space=pltpu.SMEM)


def held(x):
    return pltpu.with_memory_space_constraint(x, pltpu.VMEM)


def hbm():
    return pl.BlockSpec(memory_space=pltpu.HBM)


def unmoved(x):
    return pltpu.with_memory_space_constraint(x, pltpu.HBM)


def group(ref, j, size):
    return ref.at[pl.ds(size * j, size)]


def stream(w_hbm, w_ref, loaded):
    groups = loaded.shape[0]
    size = w_ref.shape[0] // groups
    copies = [
        pltpu.make_async_copy(group(w_hbm, j, size), group(w_ref, j, size), loaded.at[j])
        for j in range(groups)
    ]
    for copy in copies:
        copy.start()
    return copies


def load_kernel(w_ref, after_ref, out_ref, loaded):
    for copy in stream(w_ref, out_ref, loaded):
        copy.wait()


def load(w, after):
    return pl.pallas_call(
        load_kernel,
        out_shape=pltpu.VMEM(w.shape, w.dtype),
        in_specs=[hbm(), pl.BlockSpec(memory_space=pl.ANY)],
        out_specs=vmem(),
        scratch_shapes=[pltpu.SemaphoreType.DMA((8,))],
        compiler_params=pltpu.CompilerParams(vmem_limit_bytes=8 * MIB),
        cost_estimate=pl.CostEstimate(flops=0, bytes_accessed=2 * w.size, transcendentals=0),
        name="load_weights",
    )(unmoved(w), after)


def row_sums(pick, index_ref, w_ref, row):
    blocks = w_ref.shape[1]
    edge = w_ref.shape[2]
    picked = jnp.concatenate([pick(index_ref[row * blocks + k]) for k in range(blocks)], axis=1)
    return jnp.dot(picked, w_ref[row].reshape(blocks * edge, edge), preferred_element_type=F32)


def from_halves(mine_ref, other_ref):
    half = mine_ref.shape[0]

    def pick(i):
        return jnp.where(
            i < half, mine_ref[jnp.minimum(i, half - 1)], other_ref[jnp.maximum(i - half, 0)]
        )

    return pick


def from_rows(rows_ref, edge):
    return lambda i: rows_ref[:, pl.ds(pl.multiple_of(i * edge, edge), edge)]


def lower_kernel(index_ref, mine_ref, other_ref, w_ref, bias_ref, out_ref):
    pick = from_halves(mine_ref, other_ref)
    for row in range(w_ref.shape[0]):
        out_ref[row] = row_sums(pick, index_ref, w_ref, row) + bias_ref[row]


def lower_sums(low, inputs, index, w, bias):
    other = other_core(low)
    rows = w.shape[0]
    return pl.pallas_call(
        lower_kernel,
        out_shape=pltpu.VMEM((rows, low.shape[1], w.shape[3]), F32),
        in_specs=[smem()] + [vmem()] * 4,
        out_specs=vmem(),
        compiler_params=pltpu.CompilerParams(vmem_limit_bytes=8 * MIB),
        cost_estimate=pl.CostEstimate(flops=2 * w.size * 32, bytes_accessed=w.size, transcendentals=0),
        name="lower_sums",
    )(index, held(low), held(other), held(load(w, low)), held(bias))


def fresh_kernel(tick, layer_ref, index_ref, inputs_ref, w_hbm, bias_ref, out_ref, fresh_ref, w_ref, arrived, loaded):
    edge = w_ref.shape[2]

    @pl.when(layer_ref[0] == 0)
    def _():
        fresh = pltpu.make_async_copy(inputs_ref.at[tick], fresh_ref, arrived)
        fresh.start()
        copies = stream(w_hbm, w_ref, loaded)
        fresh.wait()
        pick = from_rows(fresh_ref, edge)
        for j, copy in enumerate(copies):
            copy.wait()
            for row in range(4 * j, 4 * j + 4):
                out_ref[row] = row_sums(pick, index_ref, w_ref, row) + bias_ref[row]


def fresh_scratch(inputs, w, groups):
    return [
        pltpu.VMEM(inputs.shape[1:], BF16),
        pltpu.VMEM(w.shape, w.dtype),
        pltpu.SemaphoreType.DMA,
        pltpu.SemaphoreType.DMA((groups,)),
    ]


def fresh_sums(tick, groups, layer, inputs, index, w, bias):
    return pl.pallas_call(
        functools.partial(fresh_kernel, tick),
        out_shape=pltpu.VMEM((w.shape[0], inputs.shape[1], w.shape[3]), F32),
        in_specs=[smem(), smem(), hbm(), hbm(), vmem()],
        out_specs=vmem(),
        scratch_shapes=fresh_scratch(inputs, w, groups),
        compiler_params=pltpu.CompilerParams(vmem_limit_bytes=12 * MIB),
        cost_estimate=pl.CostEstimate(flops=2 * w.size * 32, bytes_accessed=2 * w.size, transcendentals=0),
        name="fresh_sums",
    )(layer, index, unmoved(inputs), unmoved(w), held(bias))


def no_sums(low, inputs, index, w, bias):
    return jnp.zeros((w.shape[0], low.shape[1], w.shape[3]), F32)


def gates_to_state(sums, before):
    cell = jax.nn.sigmoid(sums[1]) * before + jax.nn.sigmoid(sums[0]) * jnp.tanh(sums[2])
    output = jax.nn.sigmoid(sums[3]) * jnp.tanh(cell)
    return cell, output.astype(BF16)


class Sender:
    def __init__(self, send_out, spread_ref, sent):
        self.send_out, self.spread_ref, self.sent = send_out, spread_ref, sent
        self.copies = []

    def put(self, j, output):
        for peer in range(self.spread_ref.shape[1]):
            self.spread_ref[j, peer] = output
        copy = pltpu.make_async_copy(self.spread_ref.at[j], self.send_out.at[:, j], self.sent.at[j])
        copy.start()
        self.copies.append(copy)

    def finish(self):
        for copy in self.copies:
            copy.wait()


def send_scratch(cell_shape, peers):
    per_device, row_count, edge = cell_shape
    return [pltpu.VMEM((per_device, peers, row_count, edge), BF16), pltpu.SemaphoreType.DMA((per_device,))]


def state_out(cell_shape, peers):
    per_device, row_count, edge = cell_shape
    return (
        pltpu.VMEM(cell_shape, F32),
        jax.ShapeDtypeStruct((row_count, per_device * edge), BF16),
        pltpu.HBM((peers, *cell_shape), BF16),
    )


def first_kernel(layer_ref, index_ref, inputs_ref, w_hbm, bias_ref, cell_out, rows_out, send_out, fresh_ref, w_out, arrived, loaded, spread_ref, sent):
    per_device, row_count, edge = cell_out.shape

    @pl.when(layer_ref[0] == 0)
    def _():
        fresh = pltpu.make_async_copy(inputs_ref.at[0], fresh_ref, arrived)
        fresh.start()
        copies = stream(w_hbm, w_out, loaded)
        fresh.wait()
        sender = Sender(send_out, spread_ref, sent)
        pick = from_rows(fresh_ref, edge)
        for j, copy in enumerate(copies):
            copy.wait()
            sums = [row_sums(pick, index_ref, w_out, 4 * j + g) + bias_ref[4 * j + g] for g in range(4)]
            cell_out[j], output = gates_to_state(sums, jnp.zeros((row_count, edge), F32))
            rows_out[:, j * edge:(j + 1) * edge] = output
            sender.put(j, output)
        sender.finish()

    @pl.when(layer_ref[0] != 0)
    def _():
        idle = Sender(send_out, spread_ref, sent)
        for j in range(per_device):
            idle.put(j, jnp.zeros((row_count, edge), BF16))
        for ref in (cell_out, rows_out):
            ref[...] = jnp.zeros_like(ref)
        idle.finish()


def first_step(layer, index, inputs, w, bias, per_device, peers):
    _, row_count, hidden = inputs.shape
    edge = w.shape[2]
    return pl.pallas_call(
        first_kernel,
        out_shape=state_out((per_device, row_count, edge), peers),
        in_specs=[smem(), smem(), hbm(), hbm(), vmem()],
        out_specs=(vmem(), vmem(), hbm()),
        scratch_shapes=fresh_scratch(inputs, w, per_device) + send_scratch((per_device, row_count, edge), peers),
        compiler_params=pltpu.CompilerParams(vmem_limit_bytes=12 * MIB),
        name="first_step",
    )(layer, index, unmoved(inputs), unmoved(w), held(bias))


def state_kernel(tick, step_count, layer_ref, index_ref, mine_ref, other_ref, w_ref, partial_ref, cell_ref, token_ref, cell_out, rows_out, send_out, spread_ref, sent):
    step = tick - LAG * layer_ref[0]
    active = (step >= 0) & (step < step_count)
    per_device, _, edge = cell_ref.shape

    @pl.when(active)
    def _():
        pick = from_halves(mine_ref, other_ref)
        sender = Sender(send_out, spread_ref, sent)
        for j in range(per_device):
            sums = [partial_ref[4 * j + g] + row_sums(pick, index_ref, w_ref, 4 * j + g) for g in range(4)]
            cell_out[j], output = gates_to_state(sums, cell_ref[j])
            rows_out[:, j * edge:(j + 1) * edge] = output
            sender.put(j, output)
        sender.finish()

    @pl.when(jnp.logical_not(active))
    def _():
        idle = Sender(send_out, spread_ref, sent)
        for j in range(per_device):
            idle.put(j, jnp.zeros(cell_ref.shape[1:], BF16))
        cell_out[...] = cell_ref[...]
        rows_out[...] = jnp.zeros_like(rows_out)
        idle.finish()


def state_step(tick, layer, index, state, w, partial, cell, step_count, peers, token):
    return pl.pallas_call(
        functools.partial(state_kernel, tick, step_count),
        out_shape=state_out(cell.shape, peers),
        in_specs=[smem(), smem()] + [vmem()] * 6,
        out_specs=(vmem(), vmem(), hbm()),
        scratch_shapes=send_scratch(cell.shape, peers),
        compiler_params=pltpu.CompilerParams(vmem_limit_bytes=8 * MIB),
        cost_estimate=pl.CostEstimate(flops=2 * w.size * 32, bytes_accessed=w.size, transcendentals=0),
        name="state_step",
    )(layer, index, *[held(part) for part in state], held(w), partial, cell, token)


def exchange(x, target):
    sizes = [lax.axis_size(axis) for axis in ("pipe",) + WIDTH]
    route = []
    for source in range(math.prod(sizes)):
        place, rest = [], source
        for size in reversed(sizes):
            place.insert(0, rest % size)
            rest //= size
        to = 0
        for size, at in zip(sizes, target(*place)):
            to = to * size + at % size
        route.append((source, to))
    return lax.ppermute(x, ("pipe",) + WIDTH, route)


def other_core(x):
    return exchange(x, lambda layer, y, x_at, core: (layer, y, x_at, 1 - core))


def upward(x):
    return exchange(x, lambda layer, y, x_at, core: (layer + 1, y, x_at, core))


def mark_kernel(x_ref, out_ref):
    out_ref[...] = x_ref[0, :8].astype(F32)


def mark(x, size):
    return pl.pallas_call(
        mark_kernel,
        out_shape=pltpu.VMEM((8, x.shape[2]), F32),
        in_specs=[vmem()],
        out_specs=vmem(),
        compiler_params=pltpu.CompilerParams(vmem_limit_bytes=2 * MIB),
        cost_estimate=pl.CostEstimate(flops=size, bytes_accessed=4096, transcendentals=0),
        name="mark",
    )(held(x))


def body(inputs, in_blocks, rec_blocks, in_cols, rec_cols, bias):
    layer = lax.axis_index("pipe")
    layers = lax.axis_size("pipe")
    core = lax.axis_index("core")
    step_count, row_count, hidden = inputs.shape
    _, per_device, gates, kept, edge, _ = in_blocks.shape
    total = hidden // edge
    half = total // 2
    rows = per_device * gates

    chips = lax.axis_size("y") * lax.axis_size("x")

    def place(cols):
        device = cols // per_device
        return ((device % 2) ^ core) * half + (device // 2) * per_device + cols % per_device

    in_flat = in_cols.reshape(-1)
    in_index = jnp.where(layer == 0, in_flat, place(in_flat))
    rec_index = place(rec_cols.reshape(-1))
    offsets = bias[0].reshape(gates, per_device, edge).transpose(1, 0, 2).reshape(rows, 1, edge)
    layer_ref = layer.astype(jnp.int32).reshape(1)
    w_in = in_blocks.reshape(rows, kept, edge, edge)
    w_rec = rec_blocks.reshape(rows, kept, edge, edge)

    tick_count = step_count + LAG * (layers - 1)
    steps = [tick - LAG * layer for tick in range(tick_count)]
    fed = [(layer > 0) & (step >= 0) & (step < step_count) for step in steps]
    layer_ref, fed, in_index, rec_index = lax.optimization_barrier((layer_ref, fed, in_index, rec_index))
    cell, out_rows, send = first_step(layer_ref, in_index, inputs, w_in, offsets, per_device, chips)
    arrived = {}
    outputs = [out_rows]
    for tick in range(1, tick_count):
        mine = lax.all_to_all(send, ("y", "x"), 0, 0).reshape(half, row_count, edge)
        fresh = functools.partial(fresh_sums, tick, per_device, layer_ref)
        if tick < LAG:
            partial = fresh(inputs, in_index, w_in, offsets)
        else:
            idle = (lambda low, *args: fresh(*args)) if tick < step_count else no_sums
            partial = lax.cond(fed[tick], lower_sums, idle, arrived[tick - LAG], inputs, in_index, w_in, offsets)
        mine, partial = lax.optimization_barrier((mine, partial))
        other = other_core(mine)
        if tick <= tick_count - LAG:
            arrived[tick - 1] = upward(mine)
        state = (mine, other)
        cell, out_rows, send = state_step(tick, layer_ref, rec_index, state, w_rec, partial, cell, step_count, chips, mark(mine, 1024 * w_rec.size))
        outputs.append(out_rows)
    sequence = lax.dynamic_slice_in_dim(jnp.stack(outputs), LAG * layer, step_count, 0)
    cells = cell.transpose(1, 0, 2).reshape(row_count, per_device * edge)
    return sequence[None], cells[None]


def solution(mesh):
    layers, width = mesh.devices.shape
    grid = Mesh(mesh.devices.reshape(layers, 4, width // 8, 2), ("pipe",) + WIDTH)
    return jax.shard_map(
        body,
        mesh=grid,
        in_specs=(
            P(),
            P("pipe", WIDTH, None, None, None, None),
            P("pipe", WIDTH, None, None, None, None),
            P("pipe", WIDTH, None, None),
            P("pipe", WIDTH, None, None),
            P("pipe", None, WIDTH),
        ),
        out_specs=(P("pipe", None, None, WIDTH), P("pipe", None, WIDTH)),
        check_vma=False,
    )
```

```python
import functools
import math

import jax
import jax.numpy as jnp
from jax import lax
from jax.experimental import pallas as pl
from jax.experimental.pallas import tpu as pltpu
from jax.sharding import Mesh
from jax.sharding import PartitionSpec as P

LAG = 2
F32 = jnp.float32
BF16 = jnp.bfloat16
WIDTH = ("y", "x", "core")
MIB = 2**20


def vmem():
    return pl.BlockSpec(memory_space=pltpu.VMEM)


def smem():
    return pl.BlockSpec(memory_space=pltpu.SMEM)


def held(x):
    return pltpu.with_memory_space_constraint(x, pltpu.VMEM)


def hbm():
    return pl.BlockSpec(memory_space=pltpu.HBM)


def unmoved(x):
    return pltpu.with_memory_space_constraint(x, pltpu.HBM)


def group(ref, j, size):
    return ref.at[pl.ds(size * j, size)]


def stream(w_hbm, w_ref, loaded):
    groups = loaded.shape[0]
    size = w_ref.shape[0] // groups
    copies = [
        pltpu.make_async_copy(group(w_hbm, j, size), group(w_ref, j, size), loaded.at[j])
        for j in range(groups)
    ]
    for copy in copies:
        copy.start()
    return copies


def load_kernel(w_ref, after_ref, out_ref, loaded):
    for copy in stream(w_ref, out_ref, loaded):
        copy.wait()


def load(w, after):
    return pl.pallas_call(
        load_kernel,
        out_shape=pltpu.VMEM(w.shape, w.dtype),
        in_specs=[hbm(), pl.BlockSpec(memory_space=pl.ANY)],
        out_specs=vmem(),
        scratch_shapes=[pltpu.SemaphoreType.DMA((8,))],
        compiler_params=pltpu.CompilerParams(vmem_limit_bytes=8 * MIB),
        cost_estimate=pl.CostEstimate(flops=0, bytes_accessed=2 * w.size, transcendentals=0),
        name="load_weights",
    )(unmoved(w), after)


def row_sums(pick, index_ref, w_ref, row):
    blocks = w_ref.shape[1]
    edge = w_ref.shape[2]
    if len(index_ref.shape) == 1:
        index = [index_ref[row * blocks + k] for k in range(blocks)]
    else:
        index = [index_ref[row // 4, row % 4, k] for k in range(blocks)]
    picked = jnp.concatenate([pick(i) for i in index], axis=1)
    return jnp.dot(picked, w_ref[row].reshape(blocks * edge, edge), preferred_element_type=F32)


def from_halves(mine_ref, other_ref):
    half = mine_ref.shape[0]

    def pick(i):
        return jnp.where(
            i < half, mine_ref[jnp.minimum(i, half - 1)], other_ref[jnp.maximum(i - half, 0)]
        )

    return pick


def from_rows(rows_ref, edge):
    return lambda i: rows_ref[:, pl.ds(pl.multiple_of(i * edge, edge), edge)]


def lower_kernel(index_ref, mine_ref, other_ref, w_ref, bias_ref, out_ref):
    pick = from_halves(mine_ref, other_ref)
    for row in range(w_ref.shape[0]):
        out_ref[row] = row_sums(pick, index_ref, w_ref, row) + bias_ref[row]


def lower_sums(low, inputs, index, w, bias):
    other = other_core(low)
    rows = w.shape[0]
    return pl.pallas_call(
        lower_kernel,
        out_shape=pltpu.VMEM((rows, low.shape[1], w.shape[3]), F32),
        in_specs=[smem()] + [vmem()] * 4,
        out_specs=vmem(),
        compiler_params=pltpu.CompilerParams(vmem_limit_bytes=8 * MIB),
        cost_estimate=pl.CostEstimate(flops=2 * w.size * 32, bytes_accessed=w.size, transcendentals=0),
        name="lower_sums",
    )(index, held(low), held(other), held(load(w, low)), held(bias))


def fresh_kernel(tick, layer_ref, index_ref, inputs_ref, w_hbm, bias_ref, out_ref, fresh_ref, w_ref, arrived, loaded):
    edge = w_ref.shape[2]

    @pl.when(layer_ref[0] == 0)
    def _():
        fresh = pltpu.make_async_copy(inputs_ref.at[tick], fresh_ref, arrived)
        fresh.start()
        copies = stream(w_hbm, w_ref, loaded)
        fresh.wait()
        pick = from_rows(fresh_ref, edge)
        for j, copy in enumerate(copies):
            copy.wait()
            for row in range(4 * j, 4 * j + 4):
                out_ref[row] = row_sums(pick, index_ref, w_ref, row) + bias_ref[row]


def fresh_scratch(inputs, w, groups):
    return [
        pltpu.VMEM(inputs.shape[1:], BF16),
        pltpu.VMEM(w.shape, w.dtype),
        pltpu.SemaphoreType.DMA,
        pltpu.SemaphoreType.DMA((groups,)),
    ]


def fresh_sums(tick, groups, layer, inputs, index, w, bias):
    return pl.pallas_call(
        functools.partial(fresh_kernel, tick),
        out_shape=pltpu.VMEM((w.shape[0], inputs.shape[1], w.shape[3]), F32),
        in_specs=[smem(), smem(), hbm(), hbm(), vmem()],
        out_specs=vmem(),
        scratch_shapes=fresh_scratch(inputs, w, groups),
        compiler_params=pltpu.CompilerParams(vmem_limit_bytes=12 * MIB),
        cost_estimate=pl.CostEstimate(flops=2 * w.size * 32, bytes_accessed=2 * w.size, transcendentals=0),
        name="fresh_sums",
    )(layer, index, unmoved(inputs), unmoved(w), held(bias))


def no_sums(low, inputs, index, w, bias):
    return jnp.zeros((w.shape[0], low.shape[1], w.shape[3]), F32)


def gates_to_state(sums, before):
    cell = jax.nn.sigmoid(sums[1]) * before + jax.nn.sigmoid(sums[0]) * jnp.tanh(sums[2])
    output = jax.nn.sigmoid(sums[3]) * jnp.tanh(cell)
    return cell, output.astype(BF16)


class Sender:
    def __init__(self, send_out, spread_ref, sent):
        self.send_out, self.spread_ref, self.sent = send_out, spread_ref, sent
        self.copies = []

    def put(self, j, output):
        for peer in range(self.spread_ref.shape[1]):
            self.spread_ref[j, peer] = output
        copy = pltpu.make_async_copy(self.spread_ref.at[j], self.send_out.at[:, j], self.sent.at[j])
        copy.start()
        self.copies.append(copy)

    def finish(self):
        for copy in self.copies:
            copy.wait()


def send_scratch(cell_shape, peers):
    per_device, row_count, edge = cell_shape
    return [pltpu.VMEM((per_device, peers, row_count, edge), BF16), pltpu.SemaphoreType.DMA((per_device,))]


def state_out(cell_shape, peers):
    per_device, row_count, edge = cell_shape
    return (
        pltpu.VMEM(cell_shape, F32),
        jax.ShapeDtypeStruct((row_count, per_device * edge), BF16),
        pltpu.HBM((peers, *cell_shape), BF16),
    )


def first_kernel(layer_ref, index_ref, inputs_ref, w_hbm, bias_hbm, cell_out, rows_out, send_out, bias_ref, told, fresh_ref, w_out, arrived, loaded, spread_ref, sent):
    per_device, row_count, edge = cell_out.shape

    @pl.when(layer_ref[0] == 0)
    def _():
        fresh = pltpu.make_async_copy(inputs_ref.at[0], fresh_ref, arrived)
        bias = pltpu.make_async_copy(bias_hbm, bias_ref, told)
        bias.start()
        fresh.start()
        copies = stream(w_hbm, w_out, loaded)
        bias.wait()
        fresh.wait()
        sender = Sender(send_out, spread_ref, sent)
        pick = from_rows(fresh_ref, edge)
        for j, copy in enumerate(copies):
            copy.wait()
            sums = [row_sums(pick, index_ref, w_out, 4 * j + g) + bias_ref[g:g + 1, j * edge:(j + 1) * edge] for g in range(4)]
            cell_out[j], output = gates_to_state(sums, jnp.zeros((row_count, edge), F32))
            rows_out[:, j * edge:(j + 1) * edge] = output
            sender.put(j, output)
        sender.finish()

    @pl.when(layer_ref[0] != 0)
    def _():
        idle = Sender(send_out, spread_ref, sent)
        for j in range(per_device):
            idle.put(j, jnp.zeros((row_count, edge), BF16))
        for ref in (cell_out, rows_out):
            ref[...] = jnp.zeros_like(ref)
        idle.finish()


def first_step(layer, index, inputs, w, bias, per_device, peers):
    _, row_count, hidden = inputs.shape
    edge = w.shape[2]
    return pl.pallas_call(
        first_kernel,
        out_shape=state_out((per_device, row_count, edge), peers),
        in_specs=[smem(), smem(), hbm(), hbm(), hbm()],
        out_specs=(vmem(), vmem(), hbm()),
        scratch_shapes=[pltpu.VMEM(bias.shape, F32), pltpu.SemaphoreType.DMA] + fresh_scratch(inputs, w, per_device) + send_scratch((per_device, row_count, edge), peers),
        compiler_params=pltpu.CompilerParams(vmem_limit_bytes=12 * MIB),
        name="first_step",
    )(layer, index, unmoved(inputs), unmoved(w), unmoved(bias))


def state_kernel(tick, step_count, layer_ref, index_ref, mine_ref, other_ref, w_ref, partial_ref, cell_ref, token_ref, cell_out, rows_out, send_out, spread_ref, sent):
    step = tick - LAG * layer_ref[0]
    active = (step >= 0) & (step < step_count)
    per_device, _, edge = cell_ref.shape
    last = len(cell_out.shape) == 2

    def put_cell(j, cell):
        if last:
            cell_out[:, j * edge:(j + 1) * edge] = cell
        else:
            cell_out[j] = cell

    @pl.when(active)
    def _():
        pick = from_halves(mine_ref, other_ref)
        sender = Sender(send_out, spread_ref, sent)
        for j in range(per_device):
            sums = [partial_ref[4 * j + g] + row_sums(pick, index_ref, w_ref, 4 * j + g) for g in range(4)]
            cell, output = gates_to_state(sums, cell_ref[j])
            put_cell(j, cell)
            rows_out[:, j * edge:(j + 1) * edge] = output
            if not last:
                sender.put(j, output)
        sender.finish()

    @pl.when(jnp.logical_not(active))
    def _():
        idle = Sender(send_out, spread_ref, sent)
        for j in range(per_device):
            if not last:
                idle.put(j, jnp.zeros(cell_ref.shape[1:], BF16))
            put_cell(j, cell_ref[j])
        rows_out[...] = jnp.zeros_like(rows_out)
        idle.finish()


def state_step(tick, layer, index, state, w, partial, cell, step_count, peers, token, last):
    outs = state_out(cell.shape, peers)
    if last:
        outs = (jax.ShapeDtypeStruct(outs[1].shape, F32), *outs[1:])
    return pl.pallas_call(
        functools.partial(state_kernel, tick, step_count),
        out_shape=outs,
        in_specs=[smem(), smem()] + [vmem()] * 6,
        out_specs=(vmem(), vmem(), hbm()),
        scratch_shapes=send_scratch(cell.shape, peers),
        compiler_params=pltpu.CompilerParams(vmem_limit_bytes=8 * MIB),
        cost_estimate=pl.CostEstimate(flops=2 * w.size * 32, bytes_accessed=w.size, transcendentals=0),
        name="state_step",
    )(layer, index, *[held(part) for part in state], held(w), partial, cell, token)


def exchange(x, target):
    sizes = [lax.axis_size(axis) for axis in ("pipe",) + WIDTH]
    route = []
    for source in range(math.prod(sizes)):
        place, rest = [], source
        for size in reversed(sizes):
            place.insert(0, rest % size)
            rest //= size
        to = 0
        for size, at in zip(sizes, target(*place)):
            to = to * size + at % size
        route.append((source, to))
    return lax.ppermute(x, ("pipe",) + WIDTH, route)


def other_core(x):
    return exchange(x, lambda layer, y, x_at, core: (layer, y, x_at, 1 - core))


def upward(x):
    return exchange(x, lambda layer, y, x_at, core: (layer + 1, y, x_at, core))


def mark_kernel(x_ref, out_ref):
    out_ref[...] = x_ref[0, :8].astype(F32)


def mark(x, size):
    return pl.pallas_call(
        mark_kernel,
        out_shape=pltpu.VMEM((8, x.shape[2]), F32),
        in_specs=[vmem()],
        out_specs=vmem(),
        compiler_params=pltpu.CompilerParams(vmem_limit_bytes=2 * MIB),
        cost_estimate=pl.CostEstimate(flops=size, bytes_accessed=4096, transcendentals=0),
        name="mark",
    )(held(x))


def body(inputs, in_blocks, rec_blocks, in_cols, rec_cols, bias):
    layer = lax.axis_index("pipe")
    layers = lax.axis_size("pipe")
    core = lax.axis_index("core")
    step_count, row_count, hidden = inputs.shape
    _, per_device, gates, kept, edge, _ = in_blocks.shape
    total = hidden // edge
    half = total // 2
    rows = per_device * gates

    chips = lax.axis_size("y") * lax.axis_size("x")

    def place(cols):
        device = cols // per_device
        return ((device % 2) ^ core) * half + (device // 2) * per_device + cols % per_device

    in_flat = in_cols.reshape(-1)
    in_index = jnp.where(layer == 0, in_flat, place(in_flat))
    rec_index = place(rec_cols.reshape(-1))
    offsets = bias[0].reshape(gates, per_device, edge).transpose(1, 0, 2).reshape(rows, 1, edge)
    layer_ref = layer.astype(jnp.int32).reshape(1)
    w_in = in_blocks.reshape(rows, kept, edge, edge)
    w_rec = rec_blocks.reshape(rows, kept, edge, edge)

    tick_count = step_count + LAG * (layers - 1)
    steps = [tick - LAG * layer for tick in range(tick_count)]
    fed = [(layer > 0) & (step >= 0) & (step < step_count) for step in steps]
    layer_ref, fed = lax.optimization_barrier((layer_ref, fed))
    cell, out_rows, send = first_step(layer_ref, in_cols[0], inputs, w_in, bias[0], per_device, chips)
    arrived = {}
    outputs = [out_rows]
    for tick in range(1, tick_count):
        mine = lax.all_to_all(send, ("y", "x"), 0, 0).reshape(half, row_count, edge)
        fresh = functools.partial(fresh_sums, tick, per_device, layer_ref)
        if tick < LAG:
            partial = fresh(inputs, in_index, w_in, offsets)
        else:
            idle = (lambda low, *args: fresh(*args)) if tick < step_count else no_sums
            partial = lax.cond(fed[tick], lower_sums, idle, arrived[tick - LAG], inputs, in_index, w_in, offsets)
        mine, partial = lax.optimization_barrier((mine, partial))
        other = other_core(mine)
        if tick <= tick_count - LAG:
            arrived[tick - 1] = upward(mine)
        state = (mine, other)
        token = mark(mine, 1024 * w_rec.size)
        last = tick == tick_count - 1
        cell, out_rows, send = state_step(
            tick, layer_ref, rec_index, state, w_rec, partial, cell, step_count, chips, token, last
        )
        outputs.append(out_rows)
    sequence = lax.dynamic_slice_in_dim(jnp.stack(outputs), LAG * layer, step_count, 0)
    return sequence[None], cell[None]


def solution(mesh):
    layers, width = mesh.devices.shape
    grid = Mesh(mesh.devices.reshape(layers, 4, width // 8, 2), ("pipe",) + WIDTH)
    return jax.shard_map(
        body,
        mesh=grid,
        in_specs=(
            P(),
            P("pipe", WIDTH, None, None, None, None),
            P("pipe", WIDTH, None, None, None, None),
            P("pipe", WIDTH, None, None),
            P("pipe", WIDTH, None, None),
            P("pipe", None, WIDTH),
        ),
        out_specs=(P("pipe", None, None, WIDTH), P("pipe", None, WIDTH)),
        check_vma=False,
    )
```

```python
import functools
import math

import jax
import jax.numpy as jnp
from jax import lax
from jax.experimental import pallas as pl
from jax.experimental.pallas import tpu as pltpu
from jax.sharding import Mesh
from jax.sharding import PartitionSpec as P

LAG = 2
F32 = jnp.float32
BF16 = jnp.bfloat16
WIDTH = ("y", "x", "core")
MIB = 2**20


def vmem():
    return pl.BlockSpec(memory_space=pltpu.VMEM)


def smem():
    return pl.BlockSpec(memory_space=pltpu.SMEM)


def held(x):
    return pltpu.with_memory_space_constraint(x, pltpu.VMEM)


def hbm():
    return pl.BlockSpec(memory_space=pltpu.HBM)


def unmoved(x):
    return pltpu.with_memory_space_constraint(x, pltpu.HBM)


def group(ref, j, size):
    return ref.at[pl.ds(size * j, size)]


def stream(w_hbm, w_ref, loaded):
    groups = loaded.shape[0]
    size = w_ref.shape[0] // groups
    copies = [
        pltpu.make_async_copy(group(w_hbm, j, size), group(w_ref, j, size), loaded.at[j])
        for j in range(groups)
    ]
    for copy in copies:
        copy.start()
    return copies


def load_kernel(w_ref, after_ref, out_ref, loaded):
    for copy in stream(w_ref, out_ref, loaded):
        copy.wait()


def load(w, after):
    return pl.pallas_call(
        load_kernel,
        out_shape=pltpu.VMEM(w.shape, w.dtype),
        in_specs=[hbm(), pl.BlockSpec(memory_space=pl.ANY)],
        out_specs=vmem(),
        scratch_shapes=[pltpu.SemaphoreType.DMA((8,))],
        compiler_params=pltpu.CompilerParams(vmem_limit_bytes=8 * MIB),
        cost_estimate=pl.CostEstimate(flops=0, bytes_accessed=2 * w.size, transcendentals=0),
        name="load_weights",
    )(unmoved(w), after)


def row_sums(pick, index_ref, w_ref, row):
    blocks = w_ref.shape[1]
    edge = w_ref.shape[2]
    if len(index_ref.shape) == 1:
        index = [index_ref[row * blocks + k] for k in range(blocks)]
    else:
        index = [index_ref[row // 4, row % 4, k] for k in range(blocks)]
    picked = jnp.concatenate([pick(i) for i in index], axis=1)
    return jnp.dot(picked, w_ref[row].reshape(blocks * edge, edge), preferred_element_type=F32)


def from_halves(mine_ref, other_ref):
    half = mine_ref.shape[0]

    def pick(i):
        return jnp.where(
            i < half, mine_ref[jnp.minimum(i, half - 1)], other_ref[jnp.maximum(i - half, 0)]
        )

    return pick


def from_rows(rows_ref, edge):
    return lambda i: rows_ref[:, pl.ds(pl.multiple_of(i * edge, edge), edge)]


def lower_kernel(index_ref, mine_ref, other_ref, w_ref, bias_ref, out_ref):
    pick = from_halves(mine_ref, other_ref)
    for row in range(w_ref.shape[0]):
        out_ref[row] = row_sums(pick, index_ref, w_ref, row) + bias_ref[row]


def lower_sums(low, inputs, index, w, bias):
    other = other_core(low)
    rows = w.shape[0]
    return pl.pallas_call(
        lower_kernel,
        out_shape=pltpu.VMEM((rows, low.shape[1], w.shape[3]), F32),
        in_specs=[smem()] + [vmem()] * 4,
        out_specs=vmem(),
        compiler_params=pltpu.CompilerParams(vmem_limit_bytes=8 * MIB),
        cost_estimate=pl.CostEstimate(flops=2 * w.size * 32, bytes_accessed=w.size, transcendentals=0),
        name="lower_sums",
    )(index, held(low), held(other), held(load(w, low)), held(bias))


def fresh_kernel(tick, layer_ref, index_ref, inputs_ref, w_hbm, bias_ref, out_ref, fresh_ref, w_ref, arrived, loaded):
    edge = w_ref.shape[2]

    @pl.when(layer_ref[0] == 0)
    def _():
        fresh = pltpu.make_async_copy(inputs_ref.at[tick], fresh_ref, arrived)
        fresh.start()
        copies = stream(w_hbm, w_ref, loaded)
        fresh.wait()
        pick = from_rows(fresh_ref, edge)
        for j, copy in enumerate(copies):
            copy.wait()
            for row in range(4 * j, 4 * j + 4):
                out_ref[row] = row_sums(pick, index_ref, w_ref, row) + bias_ref[row]


def fresh_scratch(inputs, w, groups):
    return [
        pltpu.VMEM(inputs.shape[1:], BF16),
        pltpu.VMEM(w.shape, w.dtype),
        pltpu.SemaphoreType.DMA,
        pltpu.SemaphoreType.DMA((groups,)),
    ]


def fresh_sums(tick, groups, layer, inputs, index, w, bias):
    return pl.pallas_call(
        functools.partial(fresh_kernel, tick),
        out_shape=pltpu.VMEM((w.shape[0], inputs.shape[1], w.shape[3]), F32),
        in_specs=[smem(), smem(), hbm(), hbm(), vmem()],
        out_specs=vmem(),
        scratch_shapes=fresh_scratch(inputs, w, groups),
        compiler_params=pltpu.CompilerParams(vmem_limit_bytes=12 * MIB),
        cost_estimate=pl.CostEstimate(flops=2 * w.size * 32, bytes_accessed=2 * w.size, transcendentals=0),
        name="fresh_sums",
    )(layer, index, unmoved(inputs), unmoved(w), held(bias))


def no_sums(low, inputs, index, w, bias):
    return jnp.zeros((w.shape[0], low.shape[1], w.shape[3]), F32)


def gates_to_state(sums, before):
    cell = jax.nn.sigmoid(sums[1]) * before + jax.nn.sigmoid(sums[0]) * jnp.tanh(sums[2])
    output = jax.nn.sigmoid(sums[3]) * jnp.tanh(cell)
    return cell, output.astype(BF16)


class Sender:
    def __init__(self, send_out, spread_ref, sent):
        self.send_out, self.spread_ref, self.sent = send_out, spread_ref, sent
        self.copies = []

    def put(self, j, output):
        for peer in range(self.spread_ref.shape[1]):
            self.spread_ref[j, peer] = output
        copy = pltpu.make_async_copy(self.spread_ref.at[j], self.send_out.at[:, j], self.sent.at[j])
        copy.start()
        self.copies.append(copy)

    def finish(self):
        for copy in self.copies:
            copy.wait()


def send_scratch(cell_shape, peers):
    per_device, row_count, edge = cell_shape
    return [pltpu.VMEM((per_device, peers, row_count, edge), BF16), pltpu.SemaphoreType.DMA((per_device,))]


def state_out(cell_shape, peers):
    per_device, row_count, edge = cell_shape
    return (
        pltpu.VMEM(cell_shape, F32),
        jax.ShapeDtypeStruct((row_count, per_device * edge), BF16),
        pltpu.HBM((peers, *cell_shape), BF16),
    )


def first_kernel(layer_ref, index_ref, inputs_ref, w_hbm, bias_hbm, cell_out, rows_out, send_out, bias_ref, told, fresh_ref, w_out, arrived, loaded, spread_ref, sent):
    per_device, row_count, edge = cell_out.shape

    @pl.when(layer_ref[0] == 0)
    def _():
        fresh = pltpu.make_async_copy(inputs_ref.at[0], fresh_ref, arrived)
        bias = pltpu.make_async_copy(bias_hbm, bias_ref, told)
        bias.start()
        fresh.start()
        copies = stream(w_hbm, w_out, loaded)
        bias.wait()
        fresh.wait()
        sender = Sender(send_out, spread_ref, sent)
        pick = from_rows(fresh_ref, edge)
        for j, copy in enumerate(copies):
            copy.wait()
            sums = [row_sums(pick, index_ref, w_out, 4 * j + g) + bias_ref[g:g + 1, j * edge:(j + 1) * edge] for g in range(4)]
            cell_out[j], output = gates_to_state(sums, jnp.zeros((row_count, edge), F32))
            rows_out[:, j * edge:(j + 1) * edge] = output
            sender.put(j, output)
        sender.finish()

    @pl.when(layer_ref[0] != 0)
    def _():
        idle = Sender(send_out, spread_ref, sent)
        for j in range(per_device):
            idle.put(j, jnp.zeros((row_count, edge), BF16))
        for ref in (cell_out, rows_out):
            ref[...] = jnp.zeros_like(ref)
        idle.finish()


def first_step(layer, index, inputs, w, bias, per_device, peers):
    _, row_count, hidden = inputs.shape
    edge = w.shape[2]
    return pl.pallas_call(
        first_kernel,
        out_shape=state_out((per_device, row_count, edge), peers),
        in_specs=[smem(), smem(), hbm(), hbm(), hbm()],
        out_specs=(vmem(), vmem(), hbm()),
        scratch_shapes=[pltpu.VMEM(bias.shape, F32), pltpu.SemaphoreType.DMA] + fresh_scratch(inputs, w, per_device) + send_scratch((per_device, row_count, edge), peers),
        compiler_params=pltpu.CompilerParams(vmem_limit_bytes=12 * MIB),
        name="first_step",
    )(layer, index, unmoved(inputs), unmoved(w), unmoved(bias))


def state_kernel(tick, step_count, index_ref, mine_ref, other_ref, w_ref, partial_ref, cell_ref, token_ref, cell_out, rows_out, send_out, spread_ref, sent):
    total = 2 * mine_ref.shape[0]
    step = tick - LAG * (index_ref[0] // total)
    active = (step >= 0) & (step < step_count)
    per_device, _, edge = cell_ref.shape
    last = len(cell_out.shape) == 2

    def put_cell(j, cell):
        if last:
            cell_out[:, j * edge:(j + 1) * edge] = cell
        else:
            cell_out[j] = cell

    @pl.when(active)
    def _():
        block = from_halves(mine_ref, other_ref)
        pick = lambda i: block(i & (total - 1))
        sender = Sender(send_out, spread_ref, sent)
        for j in range(per_device):
            sums = [partial_ref[4 * j + g] + row_sums(pick, index_ref, w_ref, 4 * j + g) for g in range(4)]
            cell, output = gates_to_state(sums, cell_ref[j])
            put_cell(j, cell)
            rows_out[:, j * edge:(j + 1) * edge] = output
            if not last:
                sender.put(j, output)
        sender.finish()

    @pl.when(jnp.logical_not(active))
    def _():
        idle = Sender(send_out, spread_ref, sent)
        for j in range(per_device):
            if not last:
                idle.put(j, jnp.zeros(cell_ref.shape[1:], BF16))
            put_cell(j, cell_ref[j])
        rows_out[...] = jnp.zeros_like(rows_out)
        idle.finish()


def state_step(tick, index, state, w, partial, cell, step_count, peers, token, last):
    outs = state_out(cell.shape, peers)
    if last:
        outs = (jax.ShapeDtypeStruct(outs[1].shape, F32), *outs[1:])
    return pl.pallas_call(
        functools.partial(state_kernel, tick, step_count),
        out_shape=outs,
        in_specs=[smem()] + [vmem()] * 6,
        out_specs=(vmem(), vmem(), hbm()),
        scratch_shapes=send_scratch(cell.shape, peers),
        compiler_params=pltpu.CompilerParams(vmem_limit_bytes=8 * MIB),
        cost_estimate=pl.CostEstimate(flops=2 * w.size * 32, bytes_accessed=w.size, transcendentals=0),
        name="state_step",
    )(index, *[held(part) for part in state], held(w), partial, cell, token)


def exchange(x, target):
    sizes = [lax.axis_size(axis) for axis in ("pipe",) + WIDTH]
    route = []
    for source in range(math.prod(sizes)):
        place, rest = [], source
        for size in reversed(sizes):
            place.insert(0, rest % size)
            rest //= size
        to = 0
        for size, at in zip(sizes, target(*place)):
            to = to * size + at % size
        route.append((source, to))
    return lax.ppermute(x, ("pipe",) + WIDTH, route)


def other_core(x):
    return exchange(x, lambda layer, y, x_at, core: (layer, y, x_at, 1 - core))


def upward(x):
    return exchange(x, lambda layer, y, x_at, core: (layer + 1, y, x_at, core))


def mark_kernel(x_ref, out_ref):
    out_ref[...] = x_ref[0, :8].astype(F32)


def mark(x, size):
    return pl.pallas_call(
        mark_kernel,
        out_shape=pltpu.VMEM((8, x.shape[2]), F32),
        in_specs=[vmem()],
        out_specs=vmem(),
        compiler_params=pltpu.CompilerParams(vmem_limit_bytes=2 * MIB),
        cost_estimate=pl.CostEstimate(flops=size, bytes_accessed=4096, transcendentals=0),
        name="mark",
    )(held(x))


def body(inputs, in_blocks, rec_blocks, in_cols, rec_cols, bias):
    layer = lax.axis_index("pipe")
    layers = lax.axis_size("pipe")
    core = lax.axis_index("core")
    step_count, row_count, hidden = inputs.shape
    _, per_device, gates, kept, edge, _ = in_blocks.shape
    total = hidden // edge
    half = total // 2
    rows = per_device * gates

    chips = lax.axis_size("y") * lax.axis_size("x")

    def place(cols):
        device = cols // per_device
        return ((device % 2) ^ core) * half + (device // 2) * per_device + cols % per_device

    in_flat = in_cols.reshape(-1)
    in_index = jnp.where(layer == 0, in_flat, place(in_flat))
    rec_index = place(rec_cols.reshape(-1)) + total * layer.astype(jnp.int32)
    offsets = bias[0].reshape(gates, per_device, edge).transpose(1, 0, 2).reshape(rows, 1, edge)
    layer_ref = layer.astype(jnp.int32).reshape(1)
    w_in = in_blocks.reshape(rows, kept, edge, edge)
    w_rec = rec_blocks.reshape(rows, kept, edge, edge)

    tick_count = step_count + LAG * (layers - 1)
    steps = [tick - LAG * layer for tick in range(tick_count)]
    fed = [(layer > 0) & (step >= 0) & (step < step_count) for step in steps]
    layer_ref, fed = lax.optimization_barrier((layer_ref, fed))
    cell, out_rows, send = first_step(layer_ref, in_cols[0], inputs, w_in, bias[0], per_device, chips)
    arrived = {}
    outputs = [out_rows]
    for tick in range(1, tick_count):
        mine = lax.all_to_all(send, ("y", "x"), 0, 0).reshape(half, row_count, edge)
        fresh = functools.partial(fresh_sums, tick, per_device, layer_ref)
        if tick < LAG:
            partial = fresh(inputs, in_index, w_in, offsets)
        else:
            idle = (lambda low, *args: fresh(*args)) if tick < step_count else no_sums
            partial = lax.cond(fed[tick], lower_sums, idle, arrived[tick - LAG], inputs, in_index, w_in, offsets)
        mine, partial = lax.optimization_barrier((mine, partial))
        other = other_core(mine)
        if tick <= tick_count - LAG:
            arrived[tick - 1] = upward(mine)
        state = (mine, other)
        token = mark(mine, 1024 * w_rec.size)
        last = tick == tick_count - 1
        cell, out_rows, send = state_step(
            tick, rec_index, state, w_rec, partial, cell, step_count, chips, token, last
        )
        outputs.append(out_rows)
    sequence = lax.dynamic_slice_in_dim(jnp.stack(outputs), LAG * layer, step_count, 0)
    return sequence[None], cell[None]


def solution(mesh):
    layers, width = mesh.devices.shape
    grid = Mesh(mesh.devices.reshape(layers, 4, width // 8, 2), ("pipe",) + WIDTH)
    return jax.shard_map(
        body,
        mesh=grid,
        in_specs=(
            P(),
            P("pipe", WIDTH, None, None, None, None),
            P("pipe", WIDTH, None, None, None, None),
            P("pipe", WIDTH, None, None),
            P("pipe", WIDTH, None, None),
            P("pipe", None, WIDTH),
        ),
        out_specs=(P("pipe", None, None, WIDTH), P("pipe", None, WIDTH)),
        check_vma=False,
    )
```
